128 devices in a mesh: dp: 2 (over x_lo), expert: 32 (over z, y, core), mp: 2 (over x_hi).
Axes of the slice: x: 4 (x_hi: 2, x_lo: 2; x = x_hi * 2 + x_lo), y: 4, z: 4, core: 2. Of those that a mesh axis runs over, the one named last changes fastest.
Arguments:
- tokens: bfloat16 [8192, 768], P(('dp', 'expert')), may hold values from -6 to 6
- cotangent: bfloat16 [8192, 768], P(('dp', 'expert')), may hold values from -6 to 6
- routes: int32 [8192, 2], P(('dp', 'expert')), may hold values from 0 to 63, all different within a row; in each aligned block of 128 rows (0 to 127, 128 to 255, ...) at most 6 rows name the same one
- gate_weights: float32 [8192, 2], P(('dp', 'expert')), may hold values from 0.5 to 1
- segments: int32 [64, 128], P(('dp', 'expert')), may hold values from 0 to 3, never falling along the last dimension, each value on 1 to 64 neighbouring positions
- buckets: int32 [128, 128], replicated, may hold values from 0 to 31
- norm_gains: bfloat16 [2, 2, 768], P(None, None, ('dp', 'expert')), may hold values from 0.5 to 1.5
- attention_in: bfloat16 [2, 768, 3, 768], P(None, ('dp', 'expert'), None, 'mp'), may hold values from -0.21875 to 0.21875
- attention_out: bfloat16 [2, 768, 768], P(None, 'mp', ('dp', 'expert')), may hold values from -0.875 to 0.875
- tables: float32 [2, 12, 32], P(None, 'mp'), may hold values from -4 to 4
- dense_in: bfloat16 [768, 2, 3072], P(('dp', 'expert'), None, 'mp'), may hold values from -0.21875 to 0.21875
- dense_out: bfloat16 [3072, 768], P('mp', ('dp', 'expert')), may hold values from -0.109375 to 0.109375
- expert_in: bfloat16 [64, 768, 2, 3072], P('expert', 'dp', None, 'mp'), may hold values from -0.21875 to 0.21875
- expert_out: bfloat16 [64, 3072, 768], P('expert', 'mp', 'dp'), may hold values from -0.4375 to 0.4375
Outputs:
- block_out: bfloat16 [8192, 768], P(('dp', 'expert'))
- tokens_grad: bfloat16 [8192, 768], P(('dp', 'expert'))
- norm_gains_grad: float32 [2, 2, 768], P(None, None, ('dp', 'expert'))
- attention_in_grad: float32 [2, 768, 3, 768], P(None, ('dp', 'expert'), None, 'mp')
- attention_out_grad: float32 [2, 768, 768], P(None, 'mp', ('dp', 'expert'))
- tables_grad: float32 [2, 12, 32], P(None, 'mp')
- dense_in_grad: float32 [768, 2, 3072], P(('dp', 'expert'), None, 'mp')
- dense_out_grad: float32 [3072, 768], P('mp', ('dp', 'expert'))
- expert_in_grad: float32 [64, 768, 2, 3072], P('expert', 'dp', None, 'mp')
- expert_out_grad: float32 [64, 3072, 768], P('expert', 'mp', 'dp')
The draws below stay inside these ranges and needn't reach their ends.
Inputs may be any that keep to these rules, and one draw needn't show every extreme that they name: `routes`: the 128 tokens of one sequence name no expert more than 6 times in all, a bound that some block reaches; a token's two experts differ. `segments`: along a sequence the numbers never fall.
All inputs are finite; a program needn't handle non-finite values.
Results may differ from the reference program's by a relative error of at most 0.025.
Values may be sent and summed in bfloat16 or wider, within the bound.
No kernel may reach another device: no remote copies, remote signals or barrier semaphores. Data moves between devices by JAX's collectives and lax.ppermute only.
A program may use at most 192 MiB of HBM per device.

```python
import math
import jax
import jax.numpy as jnp
import numpy as np
from jax import lax

D = 768
HEADS = 12
HDIM = 64
FF = 3072
EFF = 3072
BUCKETS = 32
TOK_DEV = 128
EXPERTS = 64
CAP = 6
SEQS = 64
TOKENS = 8192


def plant(entries, key, smallest, high):
    place = [jax.random.randint(jax.random.fold_in(key, axis), (), 0, length) for axis, length in enumerate(entries.shape)]
    longest = entries.shape.index(max(entries.shape))
    beside = place[:longest] + [(place[longest] + 1) % entries.shape[longest]] + place[longest + 1:]
    return entries.at[tuple(place)].set(smallest).at[tuple(beside)].set(high)


def block_scale(own_key, dims, cuts, low, high):
    factor_of, own = 1.0, jax.random.fold_in(own_key, 6)
    for axis_at, parts in cuts:
        steps = jnp.exp(jax.random.uniform(jax.random.fold_in(own, axis_at), (parts,), jnp.float32, low / len(cuts), high / len(cuts)))
        factor_of = factor_of * jnp.repeat(steps, dims[axis_at] // parts).reshape([-1 if axis == axis_at else 1 for axis in range(len(dims))])
    return factor_of


def profile(amount, total, most, skew):
    loads = [(1 << 20) // math.isqrt(grade ** skew) + 1 for grade in range(2, amount + 1)]
    surplus, counts = total - most - (amount - 1), [1] * (amount - 1)
    while surplus > 0:
        candidates = [i for i in range(amount - 1) if counts[i] < most]
        mass, budget = sum([loads[i] for i in candidates]), surplus
        for i in candidates:
            extra = min(most - counts[i], max(1, budget * loads[i] // mass), surplus)
            counts[i] = counts[i] + extra
            surplus = surplus - extra
    return np.array([most] + counts)


def uneven(stream_key, amount, total, reach, skew):
    if amount == 2:
        one = jax.random.randint(stream_key, (), max(1, total - reach), min(reach, total - 1) + 1)
        return jnp.stack([one, total - one])
    sizes = jnp.asarray(profile(amount, total, reach, skew), jnp.int32)
    pairs = (amount - 1) // 2
    giver, taker = sizes[1:1 + 2 * pairs:2], sizes[2:2 + 2 * pairs:2]
    slack = jnp.minimum(giver - 1, reach - taker)
    moved = jax.random.randint(jax.random.fold_in(stream_key, 1), (pairs,), 0, 1 << 20) % (slack + 1)
    sizes = sizes.at[1:1 + 2 * pairs:2].set(giver - moved).at[2:2 + 2 * pairs:2].set(taker + moved)
    return sizes[jax.random.permutation(jax.random.fold_in(stream_key, 2), amount)]


def deal_out(key, own, number, rows, number_of, top, most, lean):
    sequence = jax.random.permutation(key, number_of)
    heavy_load, common = load_shares(number_of, rows * top, most, lean, True), load_shares(number_of, rows * top, most, lean, False)
    places = jnp.arange(number_of)

    def named(tallies, offset_by):
        used = int((tallies > 0).sum())
        fixed = max(1, used // 4)
        moved = fixed + (places - fixed + offset_by * (used - fixed)) % max(1, number_of - fixed)
        return jnp.zeros((number_of,), jnp.int32).at[sequence[jnp.where(places < fixed, places, moved)]].set(jnp.asarray(tallies, jnp.int32))

    tallies = jnp.where(number % 4 == 0, named(heavy_load, number // 4), named(common, number - number // 4 - 1))
    mixed = jax.random.permutation(jax.random.fold_in(own, 3), number_of)
    source_of, taker = mixed[0:number_of // 2 * 2:2], mixed[1:number_of // 2 * 2:2]
    slack = jnp.minimum(tallies[source_of] - 1, most - tallies[taker]) // 2
    slack = jnp.where((source_of == sequence[0]) | (taker == sequence[0]) | (tallies[taker] == 0), 0, jnp.maximum(slack, 0))
    moved = jax.random.randint(jax.random.fold_in(own, 4), (number_of // 2,), 0, 1 << 20) % (slack + 1)
    tallies = tallies.at[source_of].add(-moved).at[taker].add(moved)
    labels = jnp.searchsorted(jnp.cumsum(tallies), jnp.arange(rows * top), side="right").astype(jnp.int32)
    grid = labels.reshape(top, rows).T
    grid = grid[jax.random.permutation(jax.random.fold_in(own, 1), rows)]
    offset_by = jax.random.randint(jax.random.fold_in(own, 2), (rows, 1), 0, top)
    return jnp.take_along_axis(grid, (jnp.arange(top)[None, :] + offset_by) % top, axis=1)


def load_shares(count, total, most, lean, full):
    weights = [(1 << 20) // math.isqrt(grade ** lean) + 1 for grade in range(1, count + 1)]
    largest = most if full else min(most, max(-(-total // count), total * weights[0] // sum(weights)))
    least = 1 if total - largest >= count - 1 else 0
    holding, rest = [largest] + [least] * (count - 1), total - largest - least * (count - 1)
    while rest > 0:
        candidates = [i for i in range(1, count) if holding[i] < largest] or [i for i in range(1, count) if holding[i] < most]
        mass, remaining = sum([weights[i] for i in candidates]), rest
        for i in candidates:
            addition = min(most - holding[i], max(1, remaining * weights[i] // mass), rest)
            holding[i] = holding[i] + addition
            rest = rest - addition
    return np.array(holding)


def normal_values(own_key, extent, scale, reach, pieces=(), held_as=jnp.bfloat16):
    values = scale * jax.random.normal(own_key, extent, jnp.float32)
    if pieces:
        values = values * block_scale(own_key, extent, pieces, -0.22, 0.18)
    return jnp.clip(values, -reach, reach).astype(held_as)


def setup_inputs(seed: int = 0) -> dict:
    streams_of = jax.random.split(jax.random.key(seed), 15)
    tokens = normal_values(streams_of[0], (TOKENS, D), 1.0, 6.0, ((0, 64),))
    cotangent = normal_values(streams_of[1], (TOKENS, D), 1.0, 6.0, ((0, 64),))
    routes_keys = jax.random.split(jax.random.fold_in(streams_of[2], 1), TOKENS // TOK_DEV)
    routes_turns = jax.random.permutation(jax.random.fold_in(streams_of[2], 3), TOKENS // TOK_DEV)
    routes = jax.vmap(lambda own, number: deal_out(jax.random.fold_in(streams_of[2], 2), own, number, TOK_DEV, EXPERTS, 2, CAP, 1))(routes_keys, routes_turns).reshape((TOKENS, 2))
    gate_weights = jnp.clip(0.5 + 0.5 * jax.random.uniform(streams_of[3], (TOKENS, 2), jnp.float32) ** block_scale(streams_of[3], (TOKENS, 2), ((0, 64),), -0.2, 0.2), 0.5, 1.0)
    segments = jax.vmap(lambda own: jnp.searchsorted(jnp.cumsum(uneven(own, 4, TOK_DEV, TOK_DEV // 2, 0)), jnp.arange(TOK_DEV), side="right"))(jax.random.split(streams_of[4], SEQS)).reshape((SEQS, TOK_DEV)).astype(jnp.int32)
    buckets = plant(jax.random.randint(streams_of[5], (TOK_DEV, TOK_DEV), 0, BUCKETS), jax.random.fold_in(streams_of[5], 1), 0, BUCKETS - 1).astype(jnp.int32)
    norm_gains = jnp.clip(1.0 + 0.1 * jax.random.normal(streams_of[6], (2, 2, D), jnp.float32), 0.5, 1.5).astype(jnp.bfloat16)
    attention_in = normal_values(streams_of[7], (2, D, 3, HEADS * HDIM), D ** -0.5, 0.21875, ((1, 64), (3, 2)))
    attention_out = normal_values(streams_of[8], (2, HEADS * HDIM, D), (HEADS * HDIM // 16) ** -0.5, 0.875, ((1, 2), (2, 64)))
    tables = normal_values(streams_of[9], (2, HEADS, BUCKETS), 1.0, 4.0, ((1, 2),), jnp.float32)
    dense_in = normal_values(streams_of[10], (D, 2, FF), D ** -0.5, 0.21875, ((0, 64), (2, 2)))
    dense_out = normal_values(streams_of[11], (FF, D), FF ** -0.5, 0.109375, ((0, 2), (1, 64)))
    expert_in = normal_values(streams_of[12], (EXPERTS, D, 2, EFF), D ** -0.5, 0.21875, ((0, 32), (1, 2), (3, 2)))
    expert_out = normal_values(streams_of[13], (EXPERTS, EFF, D), (EFF // 16) ** -0.5, 0.4375, ((0, 32), (1, 2), (2, 2)))
    return dict(tokens=tokens, cotangent=cotangent, routes=routes, gate_weights=gate_weights, segments=segments, buckets=buckets, norm_gains=norm_gains, attention_in=attention_in, attention_out=attention_out, tables=tables, dense_in=dense_in, dense_out=dense_out, expert_in=expert_in, expert_out=expert_out)


highest = lax.Precision.HIGHEST
masked_fill = -1000000000.0
epsilon = 1e-06

@jax.custom_vjp
def low(v):
    return lax.optimization_barrier(v.astype(jnp.bfloat16)).astype(jnp.float32)

@jax.custom_vjp
def low_back(v):
    return v

def low_keep(v):
    return (low(v), None)

def low_pass(kept, grad):
    return (grad,)

def back_keep(v):
    return (v, None)

def back_low(kept, grad):
    return (low(grad),)
low.defvjp(low_keep, low_pass)
low_back.defvjp(back_keep, back_low)

def both_low(operand):
    return low(low_back(operand))

def exact(pattern, first_op, second_op):
    return jnp.einsum(pattern, first_op, second_op, precision=highest)

def rms_norm(hidden, norm_gain):
    factor = lax.rsqrt(lax.optimization_barrier(jnp.mean(hidden * hidden, axis=-1, keepdims=True)) + epsilon)
    return hidden * factor * norm_gain

def attention(hidden, layer_index, norm_gains, attention_in, attention_out, tables, allowed, buckets):
    groups = hidden.shape[0]
    normed = low(rms_norm(hidden, norm_gains[layer_index, 0]))
    project = both_low(exact('gsd,dkh->gskh', normed, attention_in[layer_index]))
    project = project.reshape(groups, TOK_DEV, 3, HEADS, HDIM)
    queries = project[:, :, 0]
    keys_all = project[:, :, 1]
    values_all = project[:, :, 2]
    raw_scores = low_back(exact('gqhd,gkhd->ghqk', queries, keys_all))
    bias = tables[layer_index][:, buckets]
    scores = raw_scores * HDIM ** (-0.5) + bias[None]
    scores = jnp.where(allowed[:, None], scores, masked_fill)
    weights = low(jax.nn.softmax(scores, axis=-1))
    mixed_heads = both_low(exact('ghqk,gkhd->gqhd', weights, values_all))
    mixed_heads = mixed_heads.reshape(groups, TOK_DEV, HEADS * HDIM)
    branch = low_back(exact('gsh,hd->gsd', mixed_heads, attention_out[layer_index]))
    return hidden + branch

def dense_block(hidden, norm_gains, dense_in, dense_out):
    normed = low(rms_norm(hidden, norm_gains[0, 1]))
    gate_up = low_back(exact('gsd,dkf->gskf', normed, dense_in))
    inner_act = low(jax.nn.gelu(gate_up[:, :, 0]) * gate_up[:, :, 1])
    return hidden + low_back(exact('gsf,fd->gsd', inner_act, dense_out))

def one_expert(operands):
    expert_rows, weight_in, weight_out = operands
    gate_up = low_back(exact('rd,dkf->rkf', expert_rows, weight_in))
    inner_act = low(jax.nn.gelu(gate_up[:, 0]) * gate_up[:, 1])
    return both_low(exact('rf,fd->rd', inner_act, weight_out))

def expert_block(hidden, norm_gains, expert_in, expert_out, routes, gate_weights):
    groups = hidden.shape[0]
    normed = low(rms_norm(hidden, norm_gains[1, 1]))
    flat_routes = routes.reshape(groups, TOK_DEV * 2)
    expert_ids = jnp.arange(EXPERTS, dtype=jnp.int32)
    onehot = (flat_routes[:, :, None] == expert_ids[None, None, :]).astype(jnp.int32)
    slot_ranks = lax.optimization_barrier(jnp.sum((jnp.cumsum(onehot, axis=1) - 1) * onehot, axis=2))
    group_ids = jnp.arange(groups, dtype=jnp.int32)[:, None]
    target = ((flat_routes * groups + group_ids) * CAP + slot_ranks).reshape(-1)
    source = jnp.repeat(normed, 2, axis=1).reshape(groups * TOK_DEV * 2, D)
    buffer = jnp.zeros((EXPERTS * groups * CAP, D), normed.dtype).at[target].set(source, unique_indices=True)
    buffer = buffer.reshape(EXPERTS, groups * CAP, D)
    outputs = lax.map(jax.checkpoint(one_expert), (buffer, expert_in, expert_out))
    picked = outputs.reshape(EXPERTS * groups * CAP, D)[target].reshape(groups, TOK_DEV, 2, D)
    mixture = lax.optimization_barrier(jnp.sum(picked * gate_weights.reshape(groups, TOK_DEV, 2, 1), axis=2))
    return hidden + mixture

def reference(tokens, cotangent, routes, gate_weights, segments, buckets, norm_gains, attention_in, attention_out, tables, dense_in, dense_out, expert_in, expert_out):
    groups = tokens.shape[0] // TOK_DEV
    positions = jnp.arange(TOK_DEV, dtype=jnp.int32)
    allowed = (segments[:, :, None] == segments[:, None, :]) & (positions[None, None, :] <= positions[None, :, None])
    gate_float = gate_weights.astype(jnp.float32)

    def forward(token_float, gain_float, attn_in_float, attn_out_float, table_float, dense_in_float, dense_out_float, expert_in_float, expert_out_float):
        hidden = token_float.reshape(groups, TOK_DEV, D)
        hidden = attention(hidden, 0, gain_float, attn_in_float, attn_out_float, table_float, allowed, buckets)
        hidden = dense_block(hidden, gain_float, dense_in_float, dense_out_float)
        hidden = attention(hidden, 1, gain_float, attn_in_float, attn_out_float, table_float, allowed, buckets)
        hidden = expert_block(hidden, gain_float, expert_in_float, expert_out_float, routes, gate_float)
        return hidden.reshape(groups * TOK_DEV, D)
    primals = (tokens.astype(jnp.float32), norm_gains.astype(jnp.float32), attention_in.astype(jnp.float32), attention_out.astype(jnp.float32), tables.astype(jnp.float32), dense_in.astype(jnp.float32), dense_out.astype(jnp.float32), expert_in.astype(jnp.float32), expert_out.astype(jnp.float32))
    result, backward = jax.vjp(forward, *primals)
    gradients = backward(cotangent.astype(jnp.float32))
    return (result.astype(jnp.bfloat16), gradients[0].astype(jnp.bfloat16), gradients[1], gradients[2], gradients[3], gradients[4], gradients[5], gradients[6], gradients[7], gradients[8])
```

```python
import jax
import jax.numpy as jnp
from jax import lax
from jax.sharding import Mesh, PartitionSpec as P

HDIM = 64
SLOTS = 8
masked_fill = -1000000000.0
epsilon = 1e-06
ZY = ("z", "y")
EVERY = ("dp", "z", "y", "core")
f32 = jnp.float32
bf16 = jnp.bfloat16


def swap(value, axis):
    return lax.ppermute(value, axis, [(0, 1), (1, 0)])


def ordered(index, own, other, axis):
    first = jnp.where(index == 0, own, other)
    second = jnp.where(index == 0, other, own)
    return jnp.concatenate((first, second), axis=axis)


def mp_sum(partial):
    own = lax.optimization_barrier(partial.astype(bf16))
    return own.astype(f32) + swap(own, "mp").astype(f32)


def dot(a, b):
    return jnp.dot(a, b, preferred_element_type=f32)


def dot_nt(a, b):
    return lax.dot_general(a, b, (((1,), (1,)), ((), ())), preferred_element_type=f32)


def dot_tn(a, b):
    return lax.dot_general(a, b, (((0,), (0,)), ((), ())), preferred_element_type=f32)


def product(pattern, a, b):
    return jnp.einsum(pattern, a, b, preferred_element_type=f32)


def norm_forward(hidden, gain):
    factor = lax.rsqrt(jnp.mean(hidden * hidden, axis=-1, keepdims=True) + epsilon)
    return (hidden * factor * gain).astype(bf16), factor


def norm_backward(hidden, factor, gain, normed_grad):
    scaled = normed_grad * gain
    gain_grad = jnp.sum(normed_grad * hidden * factor, axis=0)
    middle = jnp.mean(hidden * scaled, axis=-1, keepdims=True)
    return factor * scaled - hidden * (factor * factor * factor) * middle, gain_grad


def gelu_parts(gate):
    inside = 0.7978845608028654 * (gate + 0.044715 * gate * gate * gate)
    t = jnp.tanh(inside)
    value = 0.5 * gate * (1.0 + t)
    slope = 0.5 * (1.0 + t) + 0.5 * gate * (1.0 - t * t) * (
        0.7978845608028654 * (1.0 + 3 * 0.044715 * gate * gate)
    )
    return value, slope


def attention_forward(hidden, gain, weights, bias, allowed):
    seq = hidden.shape[0]
    normed, factor = norm_forward(hidden, gain)
    split = []
    for w in weights:
        split.append(dot(normed, w[:, :576]).astype(bf16).reshape(seq, 3, 3, HDIM))
    heads = jnp.concatenate(split, axis=2)
    q, k, v = heads[:, 0], heads[:, 1], heads[:, 2]
    scores = jnp.where(allowed[None], product("qhd,khd->hqk", q, k) * HDIM**-0.5 + bias, masked_fill)
    top = jnp.max(scores, axis=-1, keepdims=True)
    shifted = jnp.exp(scores - top)
    probs = shifted / jnp.sum(shifted, axis=-1, keepdims=True)
    low = probs.astype(bf16)
    mixed = product("hqk,khd->qhd", low, v).astype(bf16)
    parts = [mixed[:, :3].reshape(seq, 192), mixed[:, 3:].reshape(seq, 192)]
    partial = dot_nt(parts[0], weights[0][:, 576:]) + dot_nt(parts[1], weights[1][:, 576:])
    return hidden + mp_sum(partial), (hidden, factor, normed, q, k, v, probs, low, parts)


def attention_backward(upstream, saved, gain, weights, onehot):
    hidden, factor, normed, q, k, v, probs, low, parts = saved
    seq = hidden.shape[0]
    branch = upstream.astype(bf16)
    out_grads = [dot_tn(branch, p) for p in parts]
    mixed_grad = jnp.concatenate(
        [dot(branch, w[:, 576:]).astype(bf16).reshape(seq, 3, HDIM) for w in weights], axis=1
    )
    v_grad = product("hqk,qhd->khd", low, mixed_grad).astype(bf16)
    probs_grad = product("qhd,khd->hqk", mixed_grad, v)
    scores_grad = probs * (probs_grad - jnp.sum(probs * probs_grad, axis=-1, keepdims=True))
    high = scores_grad.astype(bf16)
    rest = (scores_grad - high.astype(f32)).astype(bf16)
    heads = scores_grad.shape[0]
    table_grad = dot(high.reshape(heads, -1), onehot) + dot(rest.reshape(heads, -1), onehot)
    raw = (scores_grad * HDIM**-0.5).astype(bf16)
    q_grad = product("hqk,khd->qhd", raw, k).astype(bf16)
    k_grad = product("hqk,qhd->khd", raw, q).astype(bf16)
    grads = []
    partial = 0.0
    for half in range(2):
        rows = slice(3 * half, 3 * half + 3)
        proj = jnp.stack((q_grad[:, rows], k_grad[:, rows], v_grad[:, rows]), axis=1).reshape(seq, 576)
        grads.append(jnp.concatenate((dot_tn(normed, proj), out_grads[half]), axis=1))
        partial = partial + dot_nt(proj, weights[half][:, :576])
    back, gain_grad = norm_backward(hidden, factor, gain, mp_sum(partial))
    return upstream + back, gain_grad, grads, table_grad


def dense_forward(hidden, gain, weights):
    normed, factor = norm_forward(hidden, gain)
    partial = 0.0
    state = []
    for w in weights:
        gate_up = dot(normed, w[:, :1536])
        value, slope = gelu_parts(gate_up[:, :768])
        up = gate_up[:, 768:]
        inner = (value * up).astype(bf16)
        partial = partial + dot_nt(inner, w[:, 1536:])
        state.append((inner, value, slope * up))
    return hidden + mp_sum(partial), (hidden, factor, normed, state)


def dense_backward(upstream, saved, gain, weights):
    hidden, factor, normed, state = saved
    branch = upstream.astype(bf16)
    grads = []
    partial = 0.0
    for w, (inner, value, slope_up) in zip(weights, state):
        inner_grad = dot(branch, w[:, 1536:])
        both = jnp.concatenate(((inner_grad * slope_up).astype(bf16), (inner_grad * value).astype(bf16)), axis=1)
        grads.append(jnp.concatenate((dot_tn(normed, both), dot_tn(branch, inner)), axis=1))
        partial = partial + dot_nt(both, w[:, :1536])
    back, gain_grad = norm_backward(hidden, factor, gain, mp_sum(partial))
    return upstream + back, gain_grad, grads


def to_own(core, dp, own, other):
    n = own.shape[1]
    both = (own + swap(other.astype(bf16), "core").astype(f32)).astype(bf16)
    both = both.reshape(2, 16, 24, n).transpose(1, 0, 2, 3).reshape(16, 48, n)
    pieces = lax.all_to_all(both, ZY, 0, 0, tiled=True)
    rows = jnp.sum(pieces.astype(f32), axis=0)
    keep = jnp.where(dp == 0, rows[:24], rows[24:])
    send = jnp.where(dp == 0, rows[24:], rows[:24]).astype(bf16)
    rows = keep + swap(send, "dp").astype(f32)
    keep = jnp.where(core == 0, rows[:12], rows[12:])
    send = jnp.where(core == 0, rows[12:], rows[:12])
    return ordered(core, keep[None], swap(send, "core")[None], 0)


def body(
    tokens,
    cotangent,
    routes,
    gate_weights,
    segments,
    buckets,
    norm_gains,
    attention_in,
    attention_out,
    tables,
    dense_in,
    dense_out,
    expert_in,
    expert_out,
):
    core = lax.axis_index("core")
    dp = lax.axis_index("dp")
    seq, width = tokens.shape
    attn = jnp.concatenate(
        (attention_in.transpose(1, 0, 2, 3), attention_out.transpose(2, 0, 1)[:, :, None, :]), axis=2
    )
    attn = attn.reshape(12, 2, 4, 2, 192).transpose(3, 1, 0, 2, 4).reshape(2, 2, 12, 768)
    dense = jnp.concatenate((dense_in, dense_out.T[:, None, :]), axis=1)
    dense = dense.reshape(12, 3, 2, 768).transpose(2, 0, 1, 3).reshape(2, 12, 2304)
    gains = jnp.pad(norm_gains.reshape(4, 12).T, ((0, 0), (0, 124)))
    gains = jnp.broadcast_to(gains[None], (2, 12, 128))
    first = jnp.concatenate((attn[:, 0], gains), axis=2)
    rest = jnp.concatenate((dense, attn[:, 1]), axis=2)

    def spread(halves):
        own = jnp.where(core == 0, halves[0], halves[1])
        send = jnp.where(core == 0, halves[1], halves[0])
        rows = ordered(core, own, swap(send, "core"), 0)
        return ordered(dp, rows, swap(rows, "dp"), 0)

    def natural(filled):
        n = filled.shape[-1]
        return filled.reshape(16, 2, 24, n).transpose(1, 0, 2, 3).reshape(width, n)

    first = spread(first)
    first = lax.all_to_all(jnp.broadcast_to(first[None], (16, *first.shape)), ZY, 0, 0, tiled=True)
    first = natural(first)
    rest = natural(lax.all_gather(spread(rest)[None], ZY, axis=0, tiled=True))
    first_weights = (first[:, :768], swap(first[:, :768], "core"))
    rest_other = swap(rest, "core")
    dense_weights = (rest[:, :2304], rest_other[:, :2304])
    second_weights = (rest[:, 2304:], rest_other[:, 2304:])
    gains = first[:, 768:772].T.astype(f32)

    in_own = expert_in[dp]
    in_other = swap(expert_in[1 - dp], "dp")
    out_own = expert_out[dp]
    out_other = swap(expert_out[1 - dp], "dp")

    positions = jnp.arange(seq, dtype=jnp.int32)
    segment_row = segments[0]
    allowed = (segment_row[:, None] == segment_row[None, :]) & (positions[None, :] <= positions[:, None])
    bucket_ids = jnp.arange(tables.shape[2], dtype=jnp.int32)
    onehot = (buckets.reshape(-1)[:, None] == bucket_ids[None, :]).astype(bf16)
    own_tables = jnp.where(core == 0, tables, jnp.roll(tables, 3, axis=1))
    bias = jnp.einsum(
        "lhb,bx->lhx", own_tables, onehot.astype(f32).T, precision=lax.Precision.HIGHEST
    ).reshape(2, 6, seq, seq)

    experts = 64
    flat = routes.reshape(-1)
    chosen = (flat[:, None] == jnp.arange(experts, dtype=jnp.int32)[None, :]).astype(jnp.int32)
    ranks = jnp.sum((jnp.cumsum(chosen, axis=0) - 1) * chosen, axis=1)
    slots = ((flat % 2) * 32 + flat // 2) * SLOTS + ranks
    slots = slots.reshape(seq, 2)
    hits = slots[None] == jnp.arange(experts * SLOTS, dtype=jnp.int32)[:, None, None]
    fill = jnp.any(hits, axis=2).astype(bf16)
    weighted = jnp.sum(jnp.where(hits, gate_weights[None], 0.0), axis=2)
    slot_weights = jnp.sum(weighted, axis=1, keepdims=True)
    weighted_high = weighted.astype(bf16)
    weighted_rest = (weighted - weighted_high.astype(f32)).astype(bf16)

    def everywhere(rows):
        rows = rows.reshape(experts, SLOTS, width)
        return lax.all_to_all(rows, EVERY, 0, 0, tiled=True).reshape(experts * SLOTS, width)

    dy = everywhere((dot(fill, cotangent) * slot_weights).astype(bf16))

    hidden = tokens.astype(f32)
    hidden, first_state = attention_forward(hidden, gains[0], first_weights, bias[0], allowed)
    hidden, dense_state = dense_forward(hidden, gains[1], dense_weights)
    hidden, second_state = attention_forward(hidden, gains[2], second_weights, bias[1], allowed)

    half = width // 2

    def halves(rows):
        low, high = rows[:, :half], rows[:, half:]
        return jnp.where(dp == 0, low, high), jnp.where(dp == 0, high, low)

    normed, factor = norm_forward(hidden, gains[3])
    rows = everywhere(dot(fill, normed).astype(bf16))
    rows_own, rows_other = halves(rows)
    gate = dot(rows_own, in_own[:, 0]) + dot(rows_other, in_other[:, 0])
    up = dot(rows_own, in_own[:, 1]) + dot(rows_other, in_other[:, 1])
    value, slope = gelu_parts(gate)
    inner = (value * up).astype(bf16)
    y = ordered(dp, dot(inner, out_own).astype(bf16), dot(inner, out_other).astype(bf16), 1)
    y = everywhere(y)
    mixture = dot_tn(weighted_high, y) + dot_tn(weighted_rest, y)
    block_out = (hidden + mp_sum(mixture)).astype(bf16)

    dy_own, dy_other = halves(dy)
    inner_grad = dot_nt(dy_own, out_own) + dot_nt(dy_other, out_other)
    gate_grad = (inner_grad * up * slope).astype(bf16)
    up_grad = (inner_grad * value).astype(bf16)
    rows_grad = ordered(
        dp,
        (dot_nt(gate_grad, in_own[:, 0]) + dot_nt(up_grad, in_own[:, 1])).astype(bf16),
        (dot_nt(gate_grad, in_other[:, 0]) + dot_nt(up_grad, in_other[:, 1])).astype(bf16),
        1,
    )
    normed_grad = mp_sum(dot_tn(fill, everywhere(rows_grad)))
    in_send = jnp.stack((dot_tn(rows_other, gate_grad), dot_tn(rows_other, up_grad)), axis=0).astype(bf16)
    out_send = dot_tn(inner, dy_other).astype(bf16)
    in_keep = jnp.stack((dot_tn(rows_own, gate_grad), dot_tn(rows_own, up_grad)), axis=0)
    out_keep = dot_tn(inner, dy_own)
    in_recv = swap(in_send, "dp")
    out_recv = swap(out_send, "dp")
    expert_in_grad = ordered(dp, in_keep[None], in_recv[None].astype(f32), 0).transpose(0, 2, 1, 3)
    expert_out_grad = ordered(dp, out_keep[None], out_recv[None].astype(f32), 0)

    upstream = cotangent.astype(f32)
    back, gain_moe = norm_backward(hidden, factor, gains[3], normed_grad)
    upstream = upstream + back
    upstream, gain_second, second_grads, table_second = attention_backward(
        upstream, second_state, gains[2], second_weights, onehot
    )
    second_rows = to_own(core, dp, *second_grads)
    upstream, gain_dense, dense_grads = dense_backward(upstream, dense_state, gains[1], dense_weights)
    dense_rows = to_own(core, dp, *dense_grads)
    upstream, gain_first, first_grads, table_first = attention_backward(
        upstream, first_state, gains[0], first_weights, onehot
    )
    gain_columns = jnp.pad(jnp.stack((gain_first, gain_dense, gain_second, gain_moe)).T, ((0, 0), (0, 124)))
    first_grads = [jnp.concatenate((g, gain_columns), axis=1) for g in first_grads]
    first_rows = to_own(core, dp, *first_grads)

    table_grads = jnp.stack((table_first, table_second))
    table_grads = jnp.where(core == 0, table_grads, jnp.roll(table_grads, 3, axis=1))
    copies = jnp.broadcast_to(table_grads.reshape(1, 1, -1), (64, 1, table_grads.size))
    copies = lax.all_to_all(copies, EVERY, 0, 0, tiled=True)
    tables_grad = jnp.sum(copies, axis=0).reshape(table_grads.shape)

    norm_gains_grad = first_rows[0, :, 768:772].T.reshape(2, 2, 12)
    attn_rows = jnp.stack((first_rows[:, :, :768], second_rows)).reshape(2, 2, 12, 4, 192)
    attn_rows = attn_rows.transpose(0, 2, 3, 1, 4).reshape(2, 12, 4, 384)
    attention_in_grad = attn_rows[:, :, :3]
    attention_out_grad = attn_rows[:, :, 3].transpose(0, 2, 1)
    dense_rows = dense_rows.reshape(2, 12, 3, 768).transpose(1, 2, 0, 3).reshape(12, 3, 1536)
    dense_in_grad = dense_rows[:, :2]
    dense_out_grad = dense_rows[:, 2].T
    return (
        block_out,
        upstream.astype(bf16),
        norm_gains_grad,
        attention_in_grad,
        attention_out_grad,
        tables_grad,
        dense_in_grad,
        dense_out_grad,
        expert_in_grad,
        expert_out_grad,
    )


def solution(mesh):
    fine = Mesh(mesh.devices.reshape(2, 4, 4, 2, 2), ("dp", "z", "y", "core", "mp"))
    expert = ("z", "y", "core")
    rows = P(EVERY, None)
    weights = (
        P(None, None, EVERY),
        P(None, EVERY, None, "mp"),
        P(None, "mp", EVERY),
        P(None, "mp", None),
        P(EVERY, None, "mp"),
        P("mp", EVERY),
        P(expert, "dp", None, "mp"),
        P(expert, "mp", "dp"),
    )
    return jax.shard_map(
        body,
        mesh=fine,
        in_specs=(rows, rows, rows, rows, rows, P(), *weights),
        out_specs=(rows, rows, *weights),
        check_vma=False,
    )
```

```python
import functools

import jax
import jax.numpy as jnp
from jax import lax
from jax.experimental import pallas as pl
from jax.experimental.layout import Layout, with_layout_constraint
from jax.experimental.pallas import tpu as pltpu
from jax.sharding import Mesh, PartitionSpec as P

HDIM = 64
SLOTS = 8
masked_fill = -1000000000.0
epsilon = 1e-06
ZY = ("z", "y")
EVERY = ("dp", "z", "y", "core")
f32 = jnp.float32
bf16 = jnp.bfloat16


def swap(value, axis):
    return lax.ppermute(value, axis, [(0, 1), (1, 0)])


def after(value, *marks):
    return lax.optimization_barrier((value, *marks))[0]


def partner(value, dp):
    return lax.all_gather(value[None], "dp", axis=0, tiled=True)[1 - dp]


def after_each(values, *marks):
    return lax.optimization_barrier((*values, *marks))[: len(values)]


def ordered(index, own, other, axis):
    first = jnp.where(index == 0, own, other)
    second = jnp.where(index == 0, other, own)
    return jnp.concatenate((first, second), axis=axis)


def mp_pair(partial, *marks):
    own = after(partial, *marks)
    return own, swap(own, "mp")


def pair_sum(pair):
    return pair[0].astype(f32) + pair[1].astype(f32)


def dot(a, b):
    return jnp.dot(a, b, preferred_element_type=f32)


def dot_nt(a, b):
    return lax.dot_general(a, b, (((1,), (1,)), ((), ())), preferred_element_type=f32)


def dot_tn(a, b):
    return lax.dot_general(a, b, (((0,), (0,)), ((), ())), preferred_element_type=f32)


def product(pattern, a, b):
    return jnp.einsum(pattern, a, b, preferred_element_type=f32)


def norm_forward(hidden, gain):
    factor = lax.rsqrt(jnp.mean(hidden * hidden, axis=-1, keepdims=True) + epsilon)
    return (hidden * factor * gain).astype(bf16), factor


def norm_backward(hidden, factor, gain, normed_grad):
    scaled = normed_grad * gain
    gain_grad = jnp.sum(normed_grad * hidden * factor, axis=0)
    middle = jnp.mean(hidden * scaled, axis=-1, keepdims=True)
    return factor * scaled - hidden * (factor * factor * factor) * middle, gain_grad


def gelu_parts(gate):
    inside = 0.7978845608028654 * (gate + 0.044715 * gate * gate * gate)
    t = jnp.tanh(inside)
    value = 0.5 * gate * (1.0 + t)
    slope = 0.5 * (1.0 + t) + 0.5 * gate * (1.0 - t * t) * (
        0.7978845608028654 * (1.0 + 3 * 0.044715 * gate * gate)
    )
    return value, slope


SIDE = 768


def call(kernel, outs, weights, *operands):
    specs = [pl.BlockSpec((SIDE, SIDE), functools.partial(lambda k, i: (0, k), k)) for _, k in weights]
    specs += [pl.BlockSpec(x.shape, functools.partial(lambda n, i: (0,) * n, x.ndim)) for x in operands]
    shapes = [jax.ShapeDtypeStruct(shape, kind) for shape, kind in outs]
    return pl.pallas_call(
        kernel,
        grid=(1,),
        in_specs=specs,
        out_specs=[pl.BlockSpec(o.shape, functools.partial(lambda n, i: (0,) * n, len(o.shape))) for o in shapes],
        out_shape=shapes,
        compiler_params=pltpu.CompilerParams(vmem_limit_bytes=50 * 2**20),
    )(*[w for w, _ in weights], *operands)


def attention_forward_kernel(w0, w1, hidden, own, recv, gain, bias, allowed, *outs):
    part, hid, fac, normed_out, probs_out, *sides = outs
    h = hidden[...] + (own[...].astype(f32) + recv[...].astype(f32))
    hid[...] = h
    normed, factor = norm_forward(h, gain[...])
    fac[...] = factor
    normed_out[...] = normed
    keep = allowed[...] > 0.0
    partial = 0.0
    for side, w in enumerate((w0, w1)):
        proj, mixed = sides[2 * side : 2 * side + 2]
        values = dot(normed, w[...])
        proj[...] = values.astype(bf16)
        mixed[...] = jnp.zeros(mixed.shape, bf16)
        for head in range(3):
            q, k, v = (values[:, at + 64 * head : at + 64 * head + 64].astype(bf16) for at in (0, 192, 384))
            scores = jnp.where(keep, dot_nt(q, k) * HDIM**-0.5 + bias[3 * side + head], masked_fill)
            shifted = jnp.exp(scores - jnp.max(scores, axis=-1, keepdims=True))
            probs = shifted / jnp.sum(shifted, axis=-1, keepdims=True)
            probs_out[3 * side + head] = probs
            at = 576 + 64 * head
            mixed[:, at : at + 64] = dot(probs.astype(bf16), v).astype(bf16)
        partial = partial + dot_nt(mixed[...], w[...])
    part[...] = partial.astype(bf16)


def attention_forward(hidden, pair, gain, weights, bias, allowed):
    seq, width = hidden.shape
    rows = ((seq, width), bf16)
    outs = [rows, ((seq, width), f32), ((seq, 1), f32), rows, ((6, seq, seq), f32)] + [rows] * 4
    part, *saved = call(attention_forward_kernel, outs, weights, hidden, *pair, gain, bias, allowed)
    return part, saved


def norm_back(upstream, own, recv, hidden, factor, gain, upstream_out, gain_out):
    h = hidden[...]
    back, gain_grad = norm_backward(h, factor[...], gain[...], own[...].astype(f32) + recv[...].astype(f32))
    gain_out[...] = gain_grad[None]
    above = upstream[...] + back
    upstream_out[...] = above
    return above.astype(bf16)


def attention_backward_kernel(
    w0, w1, upstream, own, recv, hidden, factor, gain, normed, probs_in, proj0, mixed0, proj1, mixed1, *outs
):
    part, upstream_out, gain_out, grad_own, grad_other, scores_out, ext = outs
    branch = norm_back(upstream, own, recv, hidden, factor, gain, upstream_out, gain_out)
    partial = 0.0
    sides = ((w0, proj0, mixed0, grad_own), (w1, proj1, mixed1, grad_other))
    for side, (w, proj, mixed, grad) in enumerate(sides):
        mixed_grads = dot(branch, w[...])
        values = proj[...].astype(f32)
        ext[...] = jnp.zeros(ext.shape, bf16)
        for head in range(3):
            q, k, v = (values[:, at + 64 * head : at + 64 * head + 64].astype(bf16) for at in (0, 192, 384))
            mixed_grad = mixed_grads[:, 576 + 64 * head : 640 + 64 * head].astype(bf16)
            probs = probs_in[3 * side + head]
            probs_grad = dot_nt(mixed_grad, v)
            scores_grad = probs * (probs_grad - jnp.sum(probs * probs_grad, axis=-1, keepdims=True))
            scores_out[3 * side + head] = scores_grad
            raw = (scores_grad * HDIM**-0.5).astype(bf16)
            ext[:, 64 * head : 64 * head + 64] = dot(raw, k).astype(bf16)
            ext[:, 192 + 64 * head : 256 + 64 * head] = dot_tn(raw, q).astype(bf16)
            ext[:, 384 + 64 * head : 448 + 64 * head] = dot_tn(probs.astype(bf16), mixed_grad).astype(bf16)
        partial = partial + dot_nt(ext[...], w[...])
        grad[...] = (dot_tn(normed[...], ext[...]) + dot_tn(branch, mixed[...])).astype(grad.dtype)
    part[...] = partial.astype(bf16)


def attention_backward(upstream, pair, above, saved, weights):
    hidden, factor, normed, probs, *sides = saved
    seq, width = hidden.shape
    rows = ((seq, width), bf16)
    outs = [rows, ((seq, width), f32), ((1, width), f32), ((width, SIDE), f32), ((width, SIDE), bf16)]
    outs += [(probs.shape, f32), rows]
    part, upstream, gain_grad, own, other, scores, _ = call(
        attention_backward_kernel, outs, weights, upstream, *pair, *above, normed, probs, *sides
    )
    return part, upstream, gain_grad, (own, other), scores


def dense_forward_kernel(g0, u0, o0, g1, u1, o1, hidden, own, recv, gain, *outs):
    part, hid, fac, normed_out, *sides = outs
    h = hidden[...] + (own[...].astype(f32) + recv[...].astype(f32))
    hid[...] = h
    normed, factor = norm_forward(h, gain[...])
    fac[...] = factor
    normed_out[...] = normed
    partial = 0.0
    for side, (g, u, o) in enumerate(((g0, u0, o0), (g1, u1, o1))):
        inner, value_out, slope_out = sides[3 * side : 3 * side + 3]
        value, slope = gelu_parts(dot(normed, g[...]))
        up = dot(normed, u[...])
        inner[...] = (value * up).astype(bf16)
        value_out[...] = value
        slope_out[...] = slope * up
        partial = partial + dot_nt(inner[...], o[...])
    part[...] = partial.astype(bf16)


def dense_forward(hidden, pair, gain, weights):
    seq, width = hidden.shape
    rows, floats = ((seq, width), bf16), ((seq, width), f32)
    outs = [rows, floats, ((seq, 1), f32), rows] + [rows, floats, floats] * 2
    part, *saved = call(dense_forward_kernel, outs, weights, hidden, *pair, gain)
    return part, saved


def dense_backward_kernel(
    g0, u0, o0, g1, u1, o1, upstream, own, recv, hidden, factor, gain, normed, i0, v0, s0, i1, v1, s1, *outs
):
    part, upstream_out, gain_out, grad_own, grad_other = outs
    branch = norm_back(upstream, own, recv, hidden, factor, gain, upstream_out, gain_out)
    partial = 0.0
    sides = ((g0, u0, o0, i0, v0, s0, grad_own), (g1, u1, o1, i1, v1, s1, grad_other))
    for g, u, o, inner, value, slope_up, grad in sides:
        inner_grad = dot(branch, o[...])
        gate_grad = (inner_grad * slope_up[...]).astype(bf16)
        up_grad = (inner_grad * value[...]).astype(bf16)
        partial = partial + dot_nt(gate_grad, g[...]) + dot_nt(up_grad, u[...])
        grad[:, :SIDE] = dot_tn(normed[...], gate_grad).astype(grad.dtype)
        grad[:, SIDE : 2 * SIDE] = dot_tn(normed[...], up_grad).astype(grad.dtype)
        grad[:, 2 * SIDE :] = dot_tn(branch, inner[...]).astype(grad.dtype)
    part[...] = partial.astype(bf16)


def dense_backward(upstream, pair, above, saved, weights):
    hidden, factor, normed, *sides = saved
    seq, width = hidden.shape
    outs = [((seq, width), bf16), ((seq, width), f32), ((1, width), f32)]
    outs += [((width, 3 * SIDE), f32), ((width, 3 * SIDE), bf16)]
    part, upstream, gain_grad, own, other = call(
        dense_backward_kernel, outs, weights, upstream, *pair, *above, normed, *sides
    )
    return part, upstream, gain_grad, (own, other)


def table_gradient(scores_grad, onehot):
    flat = scores_grad.reshape(6, -1)
    high = flat.astype(bf16)
    return dot(high, onehot) + dot((flat - high.astype(f32)).astype(bf16), onehot)


def to_pieces(own, other):
    n = own.shape[1]
    both = (own + swap(other.astype(bf16), "core").astype(f32)).astype(bf16)
    return both.reshape(16, 48, n)


def over_zy(pieces):
    return lax.all_to_all(pieces, ZY, 0, 0, tiled=True)


def to_own(core, dp, pieces):
    rows = jnp.sum(pieces.astype(f32), axis=0)
    keep = jnp.where(dp == 0, rows[:24], rows[24:])
    send = jnp.where(dp == 0, rows[24:], rows[:24]).astype(bf16)
    rows = keep + swap(send, "dp").astype(f32)
    keep = jnp.where(core == 0, rows[:12], rows[12:])
    send = jnp.where(core == 0, rows[12:], rows[:12])
    return ordered(core, keep[None], swap(send, "core")[None], 0)


def body(
    tokens,
    cotangent,
    routes,
    gate_weights,
    segments,
    buckets,
    norm_gains,
    attention_in,
    attention_out,
    tables,
    dense_in,
    dense_out,
    expert_in,
    expert_out,
):
    core = lax.axis_index("core")
    dp = lax.axis_index("dp")
    seq, width = tokens.shape
    attn = jnp.concatenate(
        (attention_in.transpose(1, 0, 2, 3), attention_out.transpose(2, 0, 1)[:, :, None, :]), axis=2
    )
    attn = attn.reshape(12, 2, 4, 2, 192).transpose(3, 1, 0, 2, 4).reshape(2, 2, 12, 768)
    dense = jnp.concatenate((dense_in, dense_out.T[:, None, :]), axis=1)
    dense = dense.reshape(12, 3, 2, 768).transpose(2, 0, 1, 3).reshape(2, 12, 2304)
    gains = jnp.pad(norm_gains.reshape(4, 12).T, ((0, 0), (0, 124)))
    gains = jnp.broadcast_to(gains[None], (2, 12, 128))
    bundle = jnp.concatenate((attn[:, 0], gains, dense, attn[:, 1]), axis=2)

    def spread(halves):
        own = jnp.where(core == 0, halves[0], halves[1])
        send = jnp.where(core == 0, halves[1], halves[0])
        rows = ordered(core, own, swap(send, "core"), 0)
        return ordered(dp, rows, swap(rows, "dp"), 0)

    in_first = expert_in[1 - dp, :256]
    bundle = after(spread(bundle), in_first)
    first, rest = bundle[:, :896], bundle[:, 896:]
    filled = lax.all_to_all(jnp.broadcast_to(first[None], (16, *first.shape)), ZY, 0, 0, tiled=True)
    rest = lax.all_gather(rest[None], ZY, axis=0, tiled=True)

    place = jnp.arange(width, dtype=jnp.int32)
    place = (place // 24) % 16 * 48 + place // 384 * 24 + place % 24
    turn = (place[:, None] == jnp.arange(width, dtype=jnp.int32)[None, :]).astype(bf16)

    def arrival(values):
        return dot(values, turn).astype(bf16)

    def natural(values):
        return dot_nt(values, turn).astype(bf16)

    positions = jnp.arange(seq, dtype=jnp.int32)
    segment_row = segments[0]
    allowed = (segment_row[:, None] == segment_row[None, :]) & (positions[None, :] <= positions[:, None])
    bucket_ids = jnp.arange(tables.shape[2], dtype=jnp.int32)
    onehot = (buckets.reshape(-1)[:, None] == bucket_ids[None, :]).astype(bf16)
    own_tables = jnp.where(core == 0, tables, jnp.roll(tables, 3, axis=1))
    bias = jnp.einsum(
        "lhb,bx->lhx", own_tables, onehot.astype(f32).T, precision=lax.Precision.HIGHEST
    ).reshape(2, 6, seq, seq)

    def planes(shard):
        return with_layout_constraint(shard.transpose(1, 0, 2), Layout((0, 1, 2)))

    in_own = expert_in[dp]
    in_send = expert_in[1 - dp]
    out_own = expert_out[dp]
    out_sends = [expert_out[1 - dp, :768], expert_out[1 - dp, 768:]]
    experts = 64
    flat = routes.reshape(-1)
    chosen = (flat[:, None] == jnp.arange(experts, dtype=jnp.int32)[None, :]).astype(jnp.int32)
    ranks = jnp.sum((jnp.cumsum(chosen, axis=0) - 1) * chosen, axis=1)
    slots = ((flat % 2) * 32 + flat // 2) * SLOTS + ranks
    slots = slots.reshape(seq, 2)
    hits = slots[None] == jnp.arange(experts * SLOTS, dtype=jnp.int32)[:, None, None]
    fill = jnp.any(hits, axis=2).astype(bf16)
    weighted = jnp.sum(jnp.where(hits, gate_weights[None], 0.0), axis=2)
    slot_weights = jnp.sum(weighted, axis=1, keepdims=True)
    weighted_high = weighted.astype(bf16)
    weighted_rest = (weighted - weighted_high.astype(f32)).astype(bf16)

    def everywhere(rows):
        rows = rows.reshape(experts, SLOTS, width)
        return lax.all_to_all(rows, EVERY, 0, 0, tiled=True).reshape(experts * SLOTS, width)

    half = width // 2

    def to_slots(values):
        low, high = values[:, :half], values[:, half:]
        turned = jnp.concatenate((high, low), axis=1)
        return jnp.concatenate((dot(fill[:256], values), dot(fill[256:], turned)), axis=0)

    def from_slots(rows, *weights):
        straight = sum(dot_tn(w[:256], rows[:256]) for w in weights)
        turned = sum(dot_tn(w[256:], rows[256:]) for w in weights)
        return straight + jnp.concatenate((turned[:, half:], turned[:, :half]), axis=1)

    tokens = arrival(tokens)
    upstream = arrival(cotangent)
    slot_dy = (to_slots(cotangent) * slot_weights).astype(bf16)
    early = swap(after(in_first, first), "dp")
    ready = (early, tokens, upstream, slot_dy, fill, weighted_high, weighted_rest, onehot, bias, *out_sends)
    filled = after(filled, *ready).reshape(width, 896)
    first_weights = ((filled, 0), (swap(filled[:, :768], "core"), 0))
    gains = filled[:, 768:772].T.astype(f32)
    gains = [gains[k : k + 1] for k in range(4)]
    late = swap(after(in_send[256:], filled), "dp")

    hidden = tokens.astype(f32)
    upstream = upstream.astype(f32)
    allowed = allowed.astype(f32)
    none = jnp.zeros((seq, width), bf16)
    partial, first_state = attention_forward(hidden, (none, none), gains[0], first_weights, bias[0], allowed)
    pair = mp_pair(partial, late)
    out_first = swap(after(out_sends[0], pair[1]), "dp")
    rest = after(rest, pair[1]).reshape(width, 3072)
    rest_other = swap(rest, "core")
    dense_weights = [(w, k) for w in (rest, rest_other) for k in range(3)]
    second_weights = ((rest, 3), (rest_other, 3))
    partial, dense_state = dense_forward(first_state[0], pair, gains[1], dense_weights)
    pair = mp_pair(partial, out_first)
    out_last = swap(after(out_sends[1], pair[1]), "dp")
    partial, second_state = attention_forward(dense_state[0], pair, gains[2], second_weights, bias[1], allowed)
    hidden = second_state[0] + pair_sum(mp_pair(partial, out_last))

    normed, factor = norm_forward(hidden, gains[3])
    rows = to_slots(natural(normed)).astype(bf16).reshape(experts, SLOTS, width)
    both = jnp.concatenate((rows, slot_dy.reshape(experts, SLOTS, width)), axis=1)
    both = lax.all_to_all(both, EVERY, 0, 0, tiled=True)
    in_own, early, late, out_first, out_last = after_each((in_own, early, late, out_first, out_last), hidden)
    in_all = jnp.concatenate((planes(in_own), planes(early), planes(late)), axis=1)
    out_all = jnp.concatenate((out_own, jnp.concatenate((out_first, out_last))), axis=1)
    both = after(both, in_all, out_all)
    rows = both[:, :SLOTS].reshape(experts * SLOTS, width)
    dy = both[:, SLOTS:].reshape(experts * SLOTS, width)
    gate = dot(rows, in_all[0])
    up = dot(rows, in_all[1])
    value, slope = gelu_parts(gate)
    inner = (value * up).astype(bf16)

    inner_grad = dot_nt(dy, out_all)
    gate_grad = (inner_grad * up * slope).astype(bf16)
    up_grad = (inner_grad * value).astype(bf16)
    rows_grad = everywhere((dot_nt(gate_grad, in_all[0]) + dot_nt(up_grad, in_all[1])).astype(bf16))
    out_send = dot_tn(inner, dy[:, half:]).astype(bf16)
    in_send = jnp.stack([dot_tn(rows[:, half:], g).astype(bf16) for g in (gate_grad, up_grad)])
    in_recv = partner(in_send, dp)
    y = dot(inner, out_all).astype(bf16)
    rows_grad = after(rows_grad, in_send, out_send, y)
    pair = mp_pair(arrival(from_slots(rows_grad, fill).astype(bf16)))
    y = everywhere(after(y, pair[0]))
    partial, upstream, gain_moe, second_grads, second_scores = attention_backward(
        upstream, pair, (hidden, factor, gains[3]), second_state, second_weights
    )
    pair = mp_pair(partial)
    second_both = to_pieces(*second_grads)
    second_pieces = over_zy(second_both)
    recv, y = after_each((pair[1], y), second_both)
    pair = (pair[0], recv)
    partial, upstream, gain_second, dense_grads = dense_backward(
        upstream, pair, (*second_state[:2], gains[2]), dense_state, dense_weights
    )
    pair = mp_pair(partial)
    dense_both = to_pieces(*dense_grads)
    dense_pieces = over_zy(dense_both)
    recv, in_recv = after_each((pair[1], in_recv), dense_both)
    pair = (pair[0], recv)
    partial, upstream, gain_dense, first_grads, first_scores = attention_backward(
        upstream, pair, (*dense_state[:2], gains[1]), first_state, first_weights
    )
    pair = mp_pair(partial)
    recv, second_pieces = after_each((pair[1], second_pieces))
    pair = (pair[0], recv)
    first_both = to_pieces(*first_grads)
    out_recv = swap(after(out_send, pair[1]), "dp")
    inner, dy, rows, gate_grad, up_grad = after_each((inner, dy, rows, gate_grad, up_grad), first_both)
    in_keep = jnp.stack([dot_tn(rows[:, :half], g) for g in (gate_grad, up_grad)])
    out_keep = dot_tn(inner, dy[:, :half])
    expert_in_grad = ordered(dp, in_keep[None], in_recv[None].astype(f32), 0).transpose(0, 2, 1, 3)
    expert_out_grad = ordered(dp, out_keep[None], out_recv[None].astype(f32), 0)

    back, gain_first = norm_backward(*first_state[:2], gains[0], pair_sum(pair))
    upstream = upstream + back
    gain_grads = jnp.concatenate((gain_first[None], gain_dense, gain_second, gain_moe))
    table_grads = jnp.stack((table_gradient(first_scores, onehot), table_gradient(second_scores, onehot)))
    table_grads = jnp.where(core == 0, table_grads, jnp.roll(table_grads, 3, axis=1))
    copies = jnp.broadcast_to(table_grads.reshape(1, -1), (64, table_grads.size))
    gain_grads = gain_grads.reshape(4, 16, 2, 2, 12).transpose(2, 1, 3, 0, 4).reshape(64, 48)
    copies = jnp.concatenate((copies, gain_grads), axis=1)[:, None]
    copies = lax.all_to_all(copies, EVERY, 0, 0, tiled=True)
    mixture = arrival(from_slots(y, weighted_high, weighted_rest).astype(bf16))
    block_out = natural((hidden + pair_sum(mp_pair(mixture, first_both))).astype(bf16))
    second_rows = to_own(core, dp, second_pieces)
    dense_pieces, expert_in_grad, expert_out_grad = after_each(
        (dense_pieces, expert_in_grad, expert_out_grad), first_both, second_rows
    )
    first_pieces = over_zy(after(first_both, dense_pieces))
    dense_rows = to_own(core, dp, dense_pieces)
    first_pieces, copies, dense_rows = after_each((first_pieces, copies, dense_rows))
    first_rows = to_own(core, dp, first_pieces)
    copies = jnp.sum(copies, axis=0)[0]
    tables_grad = copies[: table_grads.size].reshape(table_grads.shape)
    norm_gains_grad = copies[table_grads.size :].reshape(2, 2, 12)
    attn_rows = jnp.stack((first_rows, second_rows)).reshape(2, 2, 12, 4, 192)
    attn_rows = attn_rows.transpose(0, 2, 3, 1, 4).reshape(2, 12, 4, 384)
    attention_in_grad = attn_rows[:, :, :3]
    attention_out_grad = attn_rows[:, :, 3].transpose(0, 2, 1)
    dense_rows = dense_rows.reshape(2, 12, 3, 768).transpose(1, 2, 0, 3).reshape(12, 3, 1536)
    dense_in_grad = dense_rows[:, :2]
    dense_out_grad = dense_rows[:, 2].T
    return (
        block_out,
        natural(upstream.astype(bf16)),
        norm_gains_grad,
        attention_in_grad,
        attention_out_grad,
        tables_grad,
        dense_in_grad,
        dense_out_grad,
        expert_in_grad,
        expert_out_grad,
    )


def solution(mesh):
    fine = Mesh(mesh.devices.reshape(2, 4, 4, 2, 2), ("dp", "z", "y", "core", "mp"))
    expert = ("z", "y", "core")
    rows = P(EVERY, None)
    weights = (
        P(None, None, EVERY),
        P(None, EVERY, None, "mp"),
        P(None, "mp", EVERY),
        P(None, "mp", None),
        P(EVERY, None, "mp"),
        P("mp", EVERY),
        P(expert, "dp", None, "mp"),
        P(expert, "mp", "dp"),
    )
    return jax.shard_map(
        body,
        mesh=fine,
        in_specs=(rows, rows, rows, rows, rows, P(), *weights),
        out_specs=(rows, rows, *weights),
        check_vma=False,
    )
```

```python
import functools

import jax
import jax.numpy as jnp
from jax import lax
from jax.experimental import pallas as pl
from jax.experimental.layout import Layout, with_layout_constraint
from jax.experimental.pallas import tpu as pltpu
from jax.sharding import Mesh, PartitionSpec as P

HDIM = 64
SLOTS = 8
masked_fill = -1000000000.0
epsilon = 1e-06
ZY = ("z", "y")
EVERY = ("dp", "z", "y", "core")
f32 = jnp.float32
bf16 = jnp.bfloat16


def swap(value, axis):
    return lax.ppermute(value, axis, [(0, 1), (1, 0)])


def after(value, *marks):
    return lax.optimization_barrier((value, *marks))[0]


def partner(value, dp):
    return lax.all_gather(value[None], "dp", axis=0, tiled=True)[1 - dp]


def after_each(values, *marks):
    return lax.optimization_barrier((*values, *marks))[: len(values)]


def ordered(index, own, other, axis):
    first = jnp.where(index == 0, own, other)
    second = jnp.where(index == 0, other, own)
    return jnp.concatenate((first, second), axis=axis)


def mp_pair(partial, *marks):
    own = after(partial, *marks)
    return own, swap(own, "mp")


def pair_sum(pair):
    return pair[0].astype(f32) + pair[1].astype(f32)


def dot(a, b):
    return jnp.dot(a, b, preferred_element_type=f32)


def dot_nt(a, b):
    return lax.dot_general(a, b, (((1,), (1,)), ((), ())), preferred_element_type=f32)


def dot_tn(a, b):
    return lax.dot_general(a, b, (((0,), (0,)), ((), ())), preferred_element_type=f32)


def product(pattern, a, b):
    return jnp.einsum(pattern, a, b, preferred_element_type=f32)


def norm_forward(hidden, gain):
    factor = lax.rsqrt(jnp.mean(hidden * hidden, axis=-1, keepdims=True) + epsilon)
    return (hidden * factor * gain).astype(bf16), factor


def norm_backward(hidden, factor, gain, normed_grad):
    scaled = normed_grad * gain
    gain_grad = jnp.sum(normed_grad * hidden * factor, axis=0)
    middle = jnp.mean(hidden * scaled, axis=-1, keepdims=True)
    return factor * scaled - hidden * (factor * factor * factor) * middle, gain_grad


def gelu_parts(gate):
    inside = 0.7978845608028654 * (gate + 0.044715 * gate * gate * gate)
    t = jnp.tanh(inside)
    value = 0.5 * gate * (1.0 + t)
    slope = 0.5 * (1.0 + t) + 0.5 * gate * (1.0 - t * t) * (
        0.7978845608028654 * (1.0 + 3 * 0.044715 * gate * gate)
    )
    return value, slope


SIDE = 768


def call(kernel, outs, weights, *operands):
    specs = [pl.BlockSpec((SIDE, SIDE), functools.partial(lambda k, i: (0, k), k)) for _, k in weights]
    specs += [pl.BlockSpec(x.shape, functools.partial(lambda n, i: (0,) * n, x.ndim)) for x in operands]
    shapes = [jax.ShapeDtypeStruct(shape, kind) for shape, kind in outs]
    return pl.pallas_call(
        kernel,
        grid=(1,),
        in_specs=specs,
        out_specs=[pl.BlockSpec(o.shape, functools.partial(lambda n, i: (0,) * n, len(o.shape))) for o in shapes],
        out_shape=shapes,
        compiler_params=pltpu.CompilerParams(vmem_limit_bytes=50 * 2**20),
    )(*[w for w, _ in weights], *operands)


def attention_forward_kernel(w0, w1, hidden, own, recv, gain, bias, allowed, *outs):
    part, hid, fac, normed_out, probs_out, *sides = outs
    h = hidden[...] + (own[...].astype(f32) + recv[...].astype(f32))
    hid[...] = h
    normed, factor = norm_forward(h, gain[...])
    fac[...] = factor
    normed_out[...] = normed
    keep = allowed[...] > 0.0
    partial = 0.0
    for side, w in enumerate((w0, w1)):
        proj, mixed = sides[2 * side : 2 * side + 2]
        values = dot(normed, w[...])
        proj[...] = values.astype(bf16)
        mixed[...] = jnp.zeros(mixed.shape, bf16)
        for head in range(3):
            q, k, v = (values[:, at + 64 * head : at + 64 * head + 64].astype(bf16) for at in (0, 192, 384))
            scores = jnp.where(keep, dot_nt(q, k) * HDIM**-0.5 + bias[3 * side + head], masked_fill)
            shifted = jnp.exp(scores - jnp.max(scores, axis=-1, keepdims=True))
            probs = shifted / jnp.sum(shifted, axis=-1, keepdims=True)
            probs_out[3 * side + head] = probs
            at = 576 + 64 * head
            mixed[:, at : at + 64] = dot(probs.astype(bf16), v).astype(bf16)
        partial = partial + dot_nt(mixed[...], w[...])
    part[...] = partial.astype(bf16)


def attention_forward(hidden, pair, gain, weights, bias, allowed):
    seq, width = hidden.shape
    rows = ((seq, width), bf16)
    outs = [rows, ((seq, width), f32), ((seq, 1), f32), rows, ((6, seq, seq), f32)] + [rows] * 4
    part, *saved = call(attention_forward_kernel, outs, weights, hidden, *pair, gain, bias, allowed)
    return part, saved


def norm_back(upstream, own, recv, hidden, factor, gain, upstream_out, gain_out):
    h = hidden[...]
    back, gain_grad = norm_backward(h, factor[...], gain[...], own[...].astype(f32) + recv[...].astype(f32))
    gain_out[...] = gain_grad[None]
    above = upstream[...] + back
    upstream_out[...] = above
    return above.astype(bf16)


def attention_backward_kernel(
    w0, w1, upstream, own, recv, hidden, factor, gain, normed, probs_in, proj0, mixed0, proj1, mixed1, *outs
):
    part, upstream_out, gain_out, grad_own, grad_other, scores_out, ext = outs
    branch = norm_back(upstream, own, recv, hidden, factor, gain, upstream_out, gain_out)
    partial = 0.0
    sides = ((w0, proj0, mixed0, grad_own), (w1, proj1, mixed1, grad_other))
    for side, (w, proj, mixed, grad) in enumerate(sides):
        mixed_grads = dot(branch, w[...])
        values = proj[...].astype(f32)
        ext[...] = jnp.zeros(ext.shape, bf16)
        for head in range(3):
            q, k, v = (values[:, at + 64 * head : at + 64 * head + 64].astype(bf16) for at in (0, 192, 384))
            mixed_grad = mixed_grads[:, 576 + 64 * head : 640 + 64 * head].astype(bf16)
            probs = probs_in[3 * side + head]
            probs_grad = dot_nt(mixed_grad, v)
            scores_grad = probs * (probs_grad - jnp.sum(probs * probs_grad, axis=-1, keepdims=True))
            scores_out[3 * side + head] = scores_grad
            raw = (scores_grad * HDIM**-0.5).astype(bf16)
            ext[:, 64 * head : 64 * head + 64] = dot(raw, k).astype(bf16)
            ext[:, 192 + 64 * head : 256 + 64 * head] = dot_tn(raw, q).astype(bf16)
            ext[:, 384 + 64 * head : 448 + 64 * head] = dot_tn(probs.astype(bf16), mixed_grad).astype(bf16)
        partial = partial + dot_nt(ext[...], w[...])
        grad[...] = (dot_tn(normed[...], ext[...]) + dot_tn(branch, mixed[...])).astype(grad.dtype)
    part[...] = partial.astype(bf16)


def attention_backward(upstream, pair, above, saved, weights):
    hidden, factor, normed, probs, *sides = saved
    seq, width = hidden.shape
    rows = ((seq, width), bf16)
    outs = [rows, ((seq, width), f32), ((1, width), f32), ((width, SIDE), f32), ((width, SIDE), bf16)]
    outs += [(probs.shape, f32), rows]
    part, upstream, gain_grad, own, other, scores, _ = call(
        attention_backward_kernel, outs, weights, upstream, *pair, *above, normed, probs, *sides
    )
    return part, upstream, gain_grad, (own, other), scores


def dense_forward_kernel(g0, u0, o0, g1, u1, o1, hidden, own, recv, gain, *outs):
    part, hid, fac, normed_out, *sides = outs
    h = hidden[...] + (own[...].astype(f32) + recv[...].astype(f32))
    hid[...] = h
    normed, factor = norm_forward(h, gain[...])
    fac[...] = factor
    normed_out[...] = normed
    partial = 0.0
    for side, (g, u, o) in enumerate(((g0, u0, o0), (g1, u1, o1))):
        inner, value_out, slope_out = sides[3 * side : 3 * side + 3]
        value, slope = gelu_parts(dot(normed, g[...]))
        up = dot(normed, u[...])
        inner[...] = (value * up).astype(bf16)
        value_out[...] = value
        slope_out[...] = slope * up
        partial = partial + dot_nt(inner[...], o[...])
    part[...] = partial.astype(bf16)


def dense_forward(hidden, pair, gain, weights):
    seq, width = hidden.shape
    rows, floats = ((seq, width), bf16), ((seq, width), f32)
    outs = [rows, floats, ((seq, 1), f32), rows] + [rows, floats, floats] * 2
    part, *saved = call(dense_forward_kernel, outs, weights, hidden, *pair, gain)
    return part, saved


def dense_backward_kernel(
    g0, u0, o0, g1, u1, o1, upstream, own, recv, hidden, factor, gain, normed, i0, v0, s0, i1, v1, s1, *outs
):
    part, upstream_out, gain_out, grad_own, grad_other = outs
    branch = norm_back(upstream, own, recv, hidden, factor, gain, upstream_out, gain_out)
    partial = 0.0
    sides = ((g0, u0, o0, i0, v0, s0, grad_own), (g1, u1, o1, i1, v1, s1, grad_other))
    for g, u, o, inner, value, slope_up, grad in sides:
        inner_grad = dot(branch, o[...])
        gate_grad = (inner_grad * slope_up[...]).astype(bf16)
        up_grad = (inner_grad * value[...]).astype(bf16)
        partial = partial + dot_nt(gate_grad, g[...]) + dot_nt(up_grad, u[...])
        grad[:, :SIDE] = dot_tn(normed[...], gate_grad).astype(grad.dtype)
        grad[:, SIDE : 2 * SIDE] = dot_tn(normed[...], up_grad).astype(grad.dtype)
        grad[:, 2 * SIDE :] = dot_tn(branch, inner[...]).astype(grad.dtype)
    part[...] = partial.astype(bf16)


def dense_backward(upstream, pair, above, saved, weights):
    hidden, factor, normed, *sides = saved
    seq, width = hidden.shape
    outs = [((seq, width), bf16), ((seq, width), f32), ((1, width), f32)]
    outs += [((width, 3 * SIDE), f32), ((width, 3 * SIDE), bf16)]
    part, upstream, gain_grad, own, other = call(
        dense_backward_kernel, outs, weights, upstream, *pair, *above, normed, *sides
    )
    return part, upstream, gain_grad, (own, other)


def table_gradient(scores_grad, onehot):
    flat = scores_grad.reshape(6, -1)
    high = flat.astype(bf16)
    return dot(high, onehot) + dot((flat - high.astype(f32)).astype(bf16), onehot)


def to_pieces(own, other):
    n = own.shape[1]
    both = (own + swap(other.astype(bf16), "core").astype(f32)).astype(bf16)
    return both.reshape(16, 48, n)


def over_zy(pieces):
    return lax.all_to_all(pieces, ZY, 0, 0, tiled=True)


def to_own(core, dp, pieces):
    rows = jnp.sum(pieces.astype(f32), axis=0)
    keep = jnp.where(dp == 0, rows[:24], rows[24:])
    send = jnp.where(dp == 0, rows[24:], rows[:24]).astype(bf16)
    rows = keep + swap(send, "dp").astype(f32)
    keep = jnp.where(core == 0, rows[:12], rows[12:])
    send = jnp.where(core == 0, rows[12:], rows[:12])
    return ordered(core, keep[None], swap(send, "core")[None], 0)


def body(
    tokens,
    cotangent,
    routes,
    gate_weights,
    segments,
    buckets,
    norm_gains,
    attention_in,
    attention_out,
    tables,
    dense_in,
    dense_out,
    expert_in,
    expert_out,
):
    core = lax.axis_index("core")
    dp = lax.axis_index("dp")
    seq, width = tokens.shape
    attn = jnp.concatenate(
        (attention_in.transpose(1, 0, 2, 3), attention_out.transpose(2, 0, 1)[:, :, None, :]), axis=2
    )
    attn = attn.reshape(12, 2, 4, 2, 192).transpose(3, 1, 0, 2, 4).reshape(2, 2, 12, 768)
    dense = jnp.concatenate((dense_in, dense_out.T[:, None, :]), axis=1)
    dense = dense.reshape(12, 3, 2, 768).transpose(2, 0, 1, 3).reshape(2, 12, 2304)
    gains = jnp.pad(norm_gains.reshape(4, 12).T, ((0, 0), (0, 124)))
    gains = jnp.broadcast_to(gains[None], (2, 12, 128))
    bundle = jnp.concatenate((attn[:, 0], gains, dense, attn[:, 1]), axis=2)

    def spread(halves):
        own = jnp.where(core == 0, halves[0], halves[1])
        send = jnp.where(core == 0, halves[1], halves[0])
        rows = ordered(core, own, swap(send, "core"), 0)
        return ordered(dp, rows, swap(rows, "dp"), 0)

    in_first = expert_in[1 - dp, :256]
    bundle = after(spread(bundle), in_first)
    first, rest = bundle[:, :896], bundle[:, 896:]
    filled = lax.all_to_all(jnp.broadcast_to(first[None], (16, *first.shape)), ZY, 0, 0, tiled=True)
    rest = lax.all_gather(rest[None], ZY, axis=0, tiled=True)

    place = jnp.arange(width, dtype=jnp.int32)
    place = (place // 24) % 16 * 48 + place // 384 * 24 + place % 24
    turn = (place[:, None] == jnp.arange(width, dtype=jnp.int32)[None, :]).astype(bf16)

    def arrival(values):
        return dot(values, turn).astype(bf16)

    def natural(values):
        return dot_nt(values, turn).astype(bf16)

    positions = jnp.arange(seq, dtype=jnp.int32)
    segment_row = segments[0]
    allowed = (segment_row[:, None] == segment_row[None, :]) & (positions[None, :] <= positions[:, None])
    bucket_ids = jnp.arange(tables.shape[2], dtype=jnp.int32)
    onehot = (buckets.reshape(-1)[:, None] == bucket_ids[None, :]).astype(bf16)
    own_tables = jnp.where(core == 0, tables, jnp.roll(tables, 3, axis=1))
    bias = jnp.einsum(
        "lhb,bx->lhx", own_tables, onehot.astype(f32).T, precision=lax.Precision.HIGHEST
    ).reshape(2, 6, seq, seq)

    def planes(shard):
        return with_layout_constraint(shard.transpose(1, 0, 2), Layout((0, 1, 2)))

    in_own = expert_in[dp]
    in_send = expert_in[1 - dp]
    out_own = expert_out[dp]
    out_sends = [expert_out[1 - dp, :768], expert_out[1 - dp, 768:]]
    experts = 64
    flat = routes.reshape(-1)
    chosen = (flat[:, None] == jnp.arange(experts, dtype=jnp.int32)[None, :]).astype(jnp.int32)
    ranks = jnp.sum((jnp.cumsum(chosen, axis=0) - 1) * chosen, axis=1)
    slots = ((flat % 2) * 32 + flat // 2) * SLOTS + ranks
    slots = slots.reshape(seq, 2)
    hits = slots[None] == jnp.arange(experts * SLOTS, dtype=jnp.int32)[:, None, None]
    fill = jnp.any(hits, axis=2).astype(bf16)
    weighted = jnp.sum(jnp.where(hits, gate_weights[None], 0.0), axis=2)
    slot_weights = jnp.sum(weighted, axis=1, keepdims=True)
    weighted_high = weighted.astype(bf16)
    weighted_rest = (weighted - weighted_high.astype(f32)).astype(bf16)

    def everywhere(rows):
        rows = rows.reshape(experts, SLOTS, width)
        return lax.all_to_all(rows, EVERY, 0, 0, tiled=True).reshape(experts * SLOTS, width)

    half = width // 2

    def to_slots(values):
        low, high = values[:, :half], values[:, half:]
        turned = jnp.concatenate((high, low), axis=1)
        return jnp.concatenate((dot(fill[:256], values), dot(fill[256:], turned)), axis=0)

    def from_slots(rows, *weights):
        straight = sum(dot_tn(w[:256], rows[:256]) for w in weights)
        turned = sum(dot_tn(w[256:], rows[256:]) for w in weights)
        return straight + jnp.concatenate((turned[:, half:], turned[:, :half]), axis=1)

    tokens = arrival(tokens)
    upstream = arrival(cotangent)
    slot_dy = (to_slots(cotangent) * slot_weights).astype(bf16)
    early = swap(after(in_first, first), "dp")
    ready = (early, tokens, upstream, slot_dy, fill, weighted_high, weighted_rest, onehot, bias, *out_sends)
    filled = after(filled, *ready).reshape(width, 896)
    first_weights = ((filled, 0), (swap(filled[:, :768], "core"), 0))
    gains = filled[:, 768:772].T.astype(f32)
    gains = [gains[k : k + 1] for k in range(4)]
    late = swap(after(in_send[256:], filled), "dp")

    hidden = tokens.astype(f32)
    upstream = upstream.astype(f32)
    allowed = allowed.astype(f32)
    none = jnp.zeros((seq, width), bf16)
    partial, first_state = attention_forward(hidden, (none, none), gains[0], first_weights, bias[0], allowed)
    pair = mp_pair(partial, late)
    out_first = swap(after(out_sends[0], pair[1]), "dp")
    rest = after(rest, pair[1]).reshape(width, 3072)
    rest_other = swap(rest, "core")
    dense_weights = [(w, k) for w in (rest, rest_other) for k in range(3)]
    second_weights = ((rest, 3), (rest_other, 3))
    partial, dense_state = dense_forward(first_state[0], pair, gains[1], dense_weights)
    pair = mp_pair(partial, out_first)
    out_last = swap(after(out_sends[1], pair[1]), "dp")
    partial, second_state = attention_forward(dense_state[0], pair, gains[2], second_weights, bias[1], allowed)
    hidden = second_state[0] + pair_sum(mp_pair(partial, out_last))

    normed, factor = norm_forward(hidden, gains[3])
    rows = to_slots(natural(normed)).astype(bf16).reshape(experts, SLOTS, width)
    both = jnp.concatenate((rows, slot_dy.reshape(experts, SLOTS, width)), axis=1)
    both = lax.all_to_all(both, EVERY, 0, 0, tiled=True)
    in_own, early, late, out_first, out_last = after_each((in_own, early, late, out_first, out_last), hidden)
    in_all = jnp.concatenate((planes(in_own), planes(early), planes(late)), axis=1)
    out_all = jnp.concatenate((out_own, jnp.concatenate((out_first, out_last))), axis=1)
    both = after(both, in_all, out_all)
    rows = both[:, :SLOTS].reshape(experts * SLOTS, width)
    dy = both[:, SLOTS:].reshape(experts * SLOTS, width)
    gate = dot(rows, in_all[0])
    up = dot(rows, in_all[1])
    value, slope = gelu_parts(gate)
    inner = (value * up).astype(bf16)

    inner_grad = dot_nt(dy, out_all)
    gate_grad = (inner_grad * up * slope).astype(bf16)
    up_grad = (inner_grad * value).astype(bf16)
    rows_grad = everywhere((dot_nt(gate_grad, in_all[0]) + dot_nt(up_grad, in_all[1])).astype(bf16))
    out_send = dot_tn(inner, dy[:, half:]).astype(bf16)
    in_send = jnp.stack([dot_tn(rows[:, half:], g).astype(bf16) for g in (gate_grad, up_grad)])
    in_recv = partner(in_send, dp)
    y = dot(inner, out_all).astype(bf16)
    rows_grad = after(rows_grad, in_send, out_send, y)
    pair = mp_pair(arrival(from_slots(rows_grad, fill).astype(bf16)))
    partial, upstream, gain_moe, second_grads, second_scores = attention_backward(
        upstream, pair, (hidden, factor, gains[3]), second_state, second_weights
    )
    pair = mp_pair(partial)
    second_both = to_pieces(*second_grads)
    second_pieces = over_zy(second_both)
    pair = (pair[0], after(pair[1], second_both))
    partial, upstream, gain_second, dense_grads = dense_backward(
        upstream, pair, (*second_state[:2], gains[2]), dense_state, dense_weights
    )
    pair = mp_pair(partial)
    dense_both = to_pieces(*dense_grads)
    dense_pieces = over_zy(dense_both)
    y = everywhere(after(y, partial))
    recv, in_recv, y = after_each((pair[1], in_recv, y), dense_both)
    pair = (pair[0], recv)
    partial, upstream, gain_dense, first_grads, first_scores = attention_backward(
        upstream, pair, (*dense_state[:2], gains[1]), first_state, first_weights
    )
    pair = mp_pair(partial)
    recv, second_pieces = after_each((pair[1], second_pieces))
    pair = (pair[0], recv)
    first_both = to_pieces(*first_grads)
    out_recv = swap(after(out_send, pair[1]), "dp")
    inner, dy, rows, gate_grad, up_grad = after_each((inner, dy, rows, gate_grad, up_grad), first_both)
    in_keep = jnp.stack([dot_tn(rows[:, :half], g) for g in (gate_grad, up_grad)])
    out_keep = dot_tn(inner, dy[:, :half])
    expert_in_grad = ordered(dp, in_keep[None], in_recv[None].astype(f32), 0).transpose(0, 2, 1, 3)
    expert_out_grad = ordered(dp, out_keep[None], out_recv[None].astype(f32), 0)

    back, gain_first = norm_backward(*first_state[:2], gains[0], pair_sum(pair))
    upstream = upstream + back
    gain_grads = jnp.concatenate((gain_first[None], gain_dense, gain_second, gain_moe))
    table_grads = jnp.stack((table_gradient(first_scores, onehot), table_gradient(second_scores, onehot)))
    table_grads = jnp.where(core == 0, table_grads, jnp.roll(table_grads, 3, axis=1))
    copies = jnp.broadcast_to(table_grads.reshape(1, -1), (64, table_grads.size))
    gain_grads = gain_grads.reshape(4, 16, 2, 2, 12).transpose(2, 1, 3, 0, 4).reshape(64, 48)
    copies = jnp.concatenate((copies, gain_grads), axis=1)[:, None]
    copies = lax.all_to_all(copies, EVERY, 0, 0, tiled=True)
    mixture = arrival(from_slots(y, weighted_high, weighted_rest).astype(bf16))
    block_out = natural((hidden + pair_sum(mp_pair(mixture, first_both))).astype(bf16))
    second_rows = to_own(core, dp, second_pieces)
    dense_pieces, expert_in_grad, expert_out_grad = after_each(
        (dense_pieces, expert_in_grad, expert_out_grad), first_both, second_rows
    )
    first_pieces = over_zy(after(first_both, dense_pieces))
    dense_rows = to_own(core, dp, dense_pieces)
    first_pieces, copies, dense_rows = after_each((first_pieces, copies, dense_rows))
    first_rows = to_own(core, dp, first_pieces)
    copies = jnp.sum(copies, axis=0)[0]
    tables_grad = copies[: table_grads.size].reshape(table_grads.shape)
    norm_gains_grad = copies[table_grads.size :].reshape(2, 2, 12)
    attn_rows = jnp.stack((first_rows, second_rows)).reshape(2, 2, 12, 4, 192)
    attn_rows = attn_rows.transpose(0, 2, 3, 1, 4).reshape(2, 12, 4, 384)
    attention_in_grad = attn_rows[:, :, :3]
    attention_out_grad = attn_rows[:, :, 3].transpose(0, 2, 1)
    dense_rows = dense_rows.reshape(2, 12, 3, 768).transpose(1, 2, 0, 3).reshape(12, 3, 1536)
    dense_in_grad = dense_rows[:, :2]
    dense_out_grad = dense_rows[:, 2].T
    return (
        block_out,
        natural(upstream.astype(bf16)),
        norm_gains_grad,
        attention_in_grad,
        attention_out_grad,
        tables_grad,
        dense_in_grad,
        dense_out_grad,
        expert_in_grad,
        expert_out_grad,
    )


def solution(mesh):
    fine = Mesh(mesh.devices.reshape(2, 4, 4, 2, 2), ("dp", "z", "y", "core", "mp"))
    expert = ("z", "y", "core")
    rows = P(EVERY, None)
    weights = (
        P(None, None, EVERY),
        P(None, EVERY, None, "mp"),
        P(None, "mp", EVERY),
        P(None, "mp", None),
        P(EVERY, None, "mp"),
        P("mp", EVERY),
        P(expert, "dp", None, "mp"),
        P(expert, "mp", "dp"),
    )
    return jax.shard_map(
        body,
        mesh=fine,
        in_specs=(rows, rows, rows, rows, rows, P(), *weights),
        out_specs=(rows, rows, *weights),
        check_vma=False,
    )
```
